32 devices in a mesh: inp: 2 (over y), wt: 4 (over x, core), out: 4 (over z).
Axes of the slice: x: 2, y: 2, z: 4, core: 2. Of those that a mesh axis runs over, the one named last changes fastest.
Arguments:
- layer_input: bfloat16 [1280, 7168], P('inp', 'wt'), may hold values from -13.5 to 13.5
- w_qkv: bfloat16 [3, 7168, 4096], P(None, 'wt', ('inp', 'out')), may hold values from -0.0625 to 0.0625
- w_out: bfloat16 [4096, 7168], P(('inp', 'out'), 'wt'), may hold values from -0.09375 to 0.09375
- cotangent: bfloat16 [1280, 7168], P('inp', 'wt'), may hold values from -6 to 6
Outputs:
- grad_input: bfloat16 [1280, 7168], P('inp', ('wt', 'out'))
- grad_qkv: bfloat16 [3, 7168, 4096], P(None, 'wt', ('inp', 'out'))
- grad_out: bfloat16 [4096, 7168], P(('inp', 'out'), 'wt')
The draws below stay inside these ranges and needn't reach their ends.
All inputs are finite; a program needn't handle non-finite values.
Results may differ from the reference program's by a relative error of at most 0.024.
Values may be sent and summed in bfloat16 or wider, within the bound.
A program may use at most 128 MiB of HBM per device.

```python
import math
import jax
import jax.numpy as jnp
from jax import lax

D = 7168
HEADS = 32
HEAD_DIM = 128
SEQ = 640
E = 4096
TOKENS = 1280


def draw_layer_input(key, part):
    first = jax.random.fold_in(key, 0)
    normal_part = jnp.clip(jax.random.normal(first, (TOKENS, D), jnp.float32), -4.5, 4.5)
    return normal_part.astype(jnp.bfloat16)


def levels(key, extent, shards, low, top_value):
    factor_of = 1.0
    for axis_at, shards_of in shards:
        draws = jax.random.uniform(jax.random.fold_in(jax.random.fold_in(key, 6), axis_at), (shards_of,), jnp.float32, low / len(shards), top_value / len(shards))
        factor_of = factor_of * jnp.repeat(jnp.exp(draws), extent[axis_at] // shards_of).reshape((-1,) + (1,) * (len(extent) - 1 - axis_at))
    return factor_of


def normal_values(own_key, shape, scale, reach, cuts=(), kind=jnp.bfloat16):
    array = jax.random.normal(own_key, shape, jnp.float32) * scale
    if len(cuts) > 0:
        array = levels(own_key, shape, cuts, -0.22, 0.18) * array
    return jnp.clip(array, min=-reach, max=reach).astype(kind)


def setup_inputs(seed: int = 0) -> dict:
    keys = jax.random.split(jax.random.key(seed), 5)
    layer_input = draw_layer_input(jax.random.fold_in(keys[4], 71), 0)
    w_qkv = normal_values(keys[1], (3, D, E), D ** -0.5, 0.0625, ((1, 4), (2, 8)))
    w_out = normal_values(keys[2], (E, D), E ** -0.5, 0.09375, ((0, 8), (1, 4)))
    cotangent = normal_values(keys[3], (TOKENS, D), 1.0, 6.0, ((0, 2), (1, 4)))
    return {"layer_input": layer_input, "w_qkv": w_qkv, "w_out": w_out, "cotangent": cotangent}


def attend(queries, key_rows, value_rows, grad_attended):
    length = queries.shape[0]
    scaling = 1.0 / math.sqrt(queries.shape[2])
    scores = jnp.einsum('qhd,khd->hqk', queries.astype(jnp.float32), key_rows.astype(jnp.float32)) * scaling
    row_index = jnp.arange(length)[:, None]
    col_index = jnp.arange(length)[None, :]
    causal = col_index <= row_index
    scores = jnp.where(causal[None], scores, -1e+30)
    largest = lax.optimization_barrier(jnp.max(scores, axis=2, keepdims=True))
    powers = jnp.exp(scores - largest)
    weights_f = powers / lax.optimization_barrier(jnp.sum(powers, axis=2, keepdims=True))
    weights_b = weights_f.astype(jnp.bfloat16)
    attended = jnp.einsum('hqk,khd->qhd', weights_b.astype(jnp.float32), value_rows.astype(jnp.float32)).astype(jnp.bfloat16)
    grad_f = grad_attended.astype(jnp.float32)
    grad_weights = jnp.einsum('qhd,khd->hqk', grad_f, value_rows.astype(jnp.float32))
    row_dots = lax.optimization_barrier(jnp.sum(grad_f * attended.astype(jnp.float32), axis=2))
    grad_scores = (weights_f * (grad_weights - jnp.transpose(row_dots)[:, :, None]) * scaling).astype(jnp.bfloat16)
    grad_query = jnp.einsum('hqk,khd->qhd', grad_scores.astype(jnp.float32), key_rows.astype(jnp.float32)).astype(jnp.bfloat16)
    grad_key = jnp.einsum('hqk,qhd->khd', grad_scores.astype(jnp.float32), queries.astype(jnp.float32)).astype(jnp.bfloat16)
    grad_value = jnp.einsum('hqk,qhd->khd', weights_b.astype(jnp.float32), grad_f).astype(jnp.bfloat16)
    return (attended, grad_query, grad_key, grad_value)

def one_sequence(running, pieces, w_qkv, w_out):
    seq_rows, seq_grad = pieces
    length = seq_rows.shape[0]
    projected = [jnp.dot(seq_rows, w_qkv[member], preferred_element_type=jnp.float32).astype(jnp.bfloat16) for member in range(3)]
    shaped = [member_rows.reshape(length, HEADS, HEAD_DIM) for member_rows in projected]
    grad_attn = jnp.dot(seq_grad, w_out.T, preferred_element_type=jnp.float32).astype(jnp.bfloat16)
    attended, grad_query, grad_key, grad_value = attend(shaped[0], shaped[1], shaped[2], grad_attn.reshape(length, HEADS, HEAD_DIM))
    grads = [member_grad.reshape(length, E) for member_grad in (grad_query, grad_key, grad_value)]
    input_grad = jnp.dot(grads[0], w_qkv[0].T, preferred_element_type=jnp.float32)
    input_grad = input_grad + jnp.dot(grads[1], w_qkv[1].T, preferred_element_type=jnp.float32)
    input_grad = input_grad + jnp.dot(grads[2], w_qkv[2].T, preferred_element_type=jnp.float32)
    qkv_terms = jnp.stack([jnp.dot(seq_rows.T, grads[member], preferred_element_type=jnp.float32) for member in range(3)]).astype(jnp.bfloat16)
    out_term = jnp.dot(attended.reshape(length, E).T, seq_grad, preferred_element_type=jnp.float32).astype(jnp.bfloat16)
    qkv_terms, out_term = lax.optimization_barrier((qkv_terms, out_term))
    running = (running[0] + qkv_terms.astype(jnp.float32), running[1] + out_term.astype(jnp.float32))
    return (running, input_grad.astype(jnp.bfloat16))

def reference(layer_input, w_qkv, w_out, cotangent):
    seq_count = TOKENS // SEQ
    stacked = (layer_input.reshape(seq_count, SEQ, D), cotangent.reshape(seq_count, SEQ, D))
    starting = (jnp.zeros((3, D, E), jnp.float32), jnp.zeros((E, D), jnp.float32))
    totals, input_grads = lax.scan(lambda running, pieces: one_sequence(running, pieces, w_qkv, w_out), starting, stacked)
    return (input_grads.reshape(TOKENS, D), totals[0].astype(jnp.bfloat16), totals[1].astype(jnp.bfloat16))
```

```python
import math

import jax
import jax.numpy as jnp
from jax import lax
from jax.sharding import PartitionSpec as P

HEAD_DIM = 128


def attend_block(queries, key_rows, value_rows, grad_attended):
    length = queries.shape[0]
    scaling = 1.0 / math.sqrt(queries.shape[2])
    scores = (
        jnp.einsum("qhd,khd->hqk", queries, key_rows, preferred_element_type=jnp.float32) * scaling
    )
    row_index = jnp.arange(length)[:, None]
    col_index = jnp.arange(length)[None, :]
    causal = col_index <= row_index
    scores = jnp.where(causal[None], scores, -1e30)
    largest = jnp.max(scores, axis=2, keepdims=True)
    powers = jnp.exp(scores - largest)
    weights_f = powers / jnp.sum(powers, axis=2, keepdims=True)
    weights_b = weights_f.astype(jnp.bfloat16)
    attended = jnp.einsum(
        "hqk,khd->qhd", weights_b, value_rows, preferred_element_type=jnp.float32
    ).astype(jnp.bfloat16)
    grad_weights = jnp.einsum(
        "qhd,khd->hqk", grad_attended, value_rows, preferred_element_type=jnp.float32
    )
    row_dots = jnp.sum(grad_attended.astype(jnp.float32) * attended.astype(jnp.float32), axis=2)
    grad_scores = (
        weights_f * (grad_weights - jnp.transpose(row_dots)[:, :, None]) * scaling
    ).astype(jnp.bfloat16)
    grad_query = jnp.einsum(
        "hqk,khd->qhd", grad_scores, key_rows, preferred_element_type=jnp.float32
    ).astype(jnp.bfloat16)
    grad_key = jnp.einsum(
        "hqk,qhd->khd", grad_scores, queries, preferred_element_type=jnp.float32
    ).astype(jnp.bfloat16)
    grad_value = jnp.einsum(
        "hqk,qhd->khd", weights_b, grad_attended, preferred_element_type=jnp.float32
    ).astype(jnp.bfloat16)
    return (attended, grad_query, grad_key, grad_value)


def local(layer_input, w_qkv, w_out, cotangent):
    qkv_block, out_block = (
        lax.all_gather(w_qkv, "inp", axis=2, tiled=True),
        lax.all_gather(w_out, "inp", axis=0, tiled=True),
    )
    wt_count = lax.axis_size("wt")
    head_cols = out_block.shape[0] // wt_count
    local_heads = head_cols // HEAD_DIM
    length = layer_input.shape[0]
    qkv_part = jnp.einsum("td,cde->tce", layer_input, qkv_block, preferred_element_type=jnp.float32)
    grad_part = jnp.einsum("td,ed->te", cotangent, out_block, preferred_element_type=jnp.float32)
    qkv_mine, grad_mine = (
        lax.psum_scatter(qkv_part, "wt", scatter_dimension=2, tiled=True),
        lax.psum_scatter(grad_part, "wt", scatter_dimension=1, tiled=True),
    )
    projected = qkv_mine.astype(jnp.bfloat16)
    queries = projected[:, 0].reshape(length, local_heads, HEAD_DIM)
    key_rows = projected[:, 1].reshape(length, local_heads, HEAD_DIM)
    value_rows = projected[:, 2].reshape(length, local_heads, HEAD_DIM)
    grad_attn = grad_mine.astype(jnp.bfloat16).reshape(length, local_heads, HEAD_DIM)
    attended, grad_query, grad_key, grad_value = attend_block(
        queries, key_rows, value_rows, grad_attn
    )
    grad_rows = jnp.stack([grad_query, grad_key, grad_value], axis=1).reshape(length, 3, head_cols)
    attended_rows = attended.reshape(length, head_cols)
    grad_all, attended_all = (
        lax.all_gather(grad_rows, "wt", axis=2, tiled=True),
        lax.all_gather(attended_rows, "wt", axis=1, tiled=True),
    )
    partial_input = jnp.einsum(
        "tce,cde->td", grad_all, qkv_block, preferred_element_type=jnp.float32
    )
    grad_input = lax.psum_scatter(partial_input, "out", scatter_dimension=1, tiled=True).astype(
        jnp.bfloat16
    )
    qkv_term = jnp.einsum("td,tce->cde", layer_input, grad_all, preferred_element_type=jnp.float32)
    out_term = jnp.einsum("te,td->ed", attended_all, cotangent, preferred_element_type=jnp.float32)
    qkv_total = lax.psum_scatter(
        qkv_term.astype(jnp.bfloat16), "inp", scatter_dimension=2, tiled=True
    )
    out_total = lax.psum_scatter(
        out_term.astype(jnp.bfloat16), "inp", scatter_dimension=0, tiled=True
    )
    return (grad_input, qkv_total, out_total)


BF = jnp.bfloat16
F32 = jnp.float32


def dot(a, b, dims):
    return lax.dot_general(a, b, (dims, ((), ())), preferred_element_type=F32)


def fetch_other(block, parts):
    out_at = lax.axis_index("out")
    out_count = lax.axis_size("out")
    parity = lax.rem(out_at, 2)
    half = block.shape[0] // 2
    rows = half // parts
    swap = [(0, 1), (1, 0)]
    pair = [(z, z ^ 1) for z in range(out_count)]
    got, shared = [], []
    for k in range(parts):
        piece = lax.dynamic_slice_in_dim(block, parity * half + k * rows, rows, 0)
        mine = lax.ppermute(piece, "inp", swap)
        got.append(mine)
        shared.append(lax.ppermute(mine, "out", pair))
    return jnp.where(
        parity == 0, jnp.concatenate(got + shared, 0), jnp.concatenate(shared + got, 0)
    )


def attend_one(queries, keys, values, grad_attended):
    result = attend_block(
        queries[:, None], keys[:, None], values[:, None], grad_attended[:, None]
    )
    return [r[:, 0] for r in result]


CORE = [(0, 1), (1, 0), (2, 3), (3, 2)]
ACROSS = [(0, 2), (2, 0), (1, 3), (3, 1)]


def head_work(rows, grad_rows, w_qkv, w_out):
    wt = lax.axis_index("wt")
    x_at, core = wt // 2, lax.rem(wt, 2)
    parts = [dot(rows, w_qkv[c], ((1,), (0,))).astype(BF) for c in range(3)]
    parts.append(dot(grad_rows, w_out, ((1,), (1,))).astype(BF))
    n = HEAD_DIM
    heads = [jnp.concatenate([p[:, h * n : (h + 1) * n] for p in parts], 1) for h in range(4)]
    even, odd = jnp.stack([heads[0], heads[2]]), jnp.stack([heads[1], heads[3]])
    came = lax.ppermute(jnp.where(core == 0, odd, even), "wt", CORE)
    total = jnp.where(core == 0, even, odd).astype(F32) + came.astype(F32)
    away = jnp.where(x_at == 0, total[1], total[0]).astype(BF)
    mine = jnp.where(x_at == 0, total[0], total[1])
    mine = (mine + lax.ppermute(away, "wt", ACROSS).astype(F32)).astype(BF)
    q, k, v, g = [mine[:, j * n : (j + 1) * n] for j in range(4)]
    attended, gq, gk, gv = attend_one(q, k, v, g)
    one = jnp.concatenate([gq, gk, gv, attended], 1)
    two = lax.ppermute(one, "wt", ACROSS)
    pair = jnp.where(x_at == 0, jnp.stack([one, two]), jnp.stack([two, one]))
    other = lax.ppermute(pair, "wt", CORE)
    even = jnp.where(core == 0, pair, other)
    odd = jnp.where(core == 0, other, pair)
    heads = [even[0], odd[0], even[1], odd[1]]
    return [jnp.concatenate([h[:, j * n : (j + 1) * n] for h in heads], 1) for j in range(4)]


def input_part(grads, w_qkv):
    total = sum(dot(grads[c], w_qkv[c], ((1,), (1,))) for c in range(3)).astype(BF)
    return lax.psum_scatter(total, "out", scatter_dimension=1, tiled=True)


def local_fast(layer_input, w_qkv, w_out, cotangent):
    cot_other = fetch_other(cotangent, 2)
    rows_other = fetch_other(layer_input, 2)
    own = head_work(layer_input, cotangent, w_qkv, w_out)
    own_input = input_part(own, w_qkv)
    far = head_work(rows_other, cot_other, w_qkv, w_out)
    far_input = input_part(far, w_qkv)
    back = lax.ppermute(far_input, "inp", [(0, 1), (1, 0)])
    terms = []
    for acts, cots, grads in ((layer_input, cotangent, own), (rows_other, cot_other, far)):
        qkv = jnp.stack([dot(acts, grads[c], ((0,), (0,))) for c in range(3)]).astype(BF)
        terms.append((qkv, dot(grads[3], cots, ((0,), (0,))).astype(BF)))
    grad_qkv = (terms[0][0].astype(F32) + terms[1][0].astype(F32)).astype(BF)
    grad_out = (terms[0][1].astype(F32) + terms[1][1].astype(F32)).astype(BF)
    grad_input = (own_input.astype(F32) + back.astype(F32)).astype(BF)
    return grad_input, grad_qkv, grad_out


def solution(mesh):
    sizes = dict(mesh.shape)
    fits = sizes["inp"] == 2 and sizes["wt"] == 4 and sizes["out"] % 2 == 0
    return jax.shard_map(
        local_fast if fits else local,
        mesh=mesh,
        in_specs=(
            P("inp", "wt"),
            P(None, "wt", ("inp", "out")),
            P(("inp", "out"), "wt"),
            P("inp", "wt"),
        ),
        out_specs=(P("inp", ("wt", "out")), P(None, "wt", ("inp", "out")), P(("inp", "out"), "wt")),
        check_vma=False,
    )
```

```python
import math

import jax
import jax.numpy as jnp
from jax import lax
from jax.experimental import pallas as pl
from jax.experimental.pallas import tpu as pltpu
from jax.sharding import PartitionSpec as P

HEAD_DIM = 128


def attend_block(queries, key_rows, value_rows, grad_attended):
    length = queries.shape[0]
    scaling = 1.0 / math.sqrt(queries.shape[2])
    scores = (
        jnp.einsum("qhd,khd->hqk", queries, key_rows, preferred_element_type=jnp.float32) * scaling
    )
    row_index = jnp.arange(length)[:, None]
    col_index = jnp.arange(length)[None, :]
    causal = col_index <= row_index
    scores = jnp.where(causal[None], scores, -1e30)
    largest = jnp.max(scores, axis=2, keepdims=True)
    powers = jnp.exp(scores - largest)
    weights_f = powers / jnp.sum(powers, axis=2, keepdims=True)
    weights_b = weights_f.astype(jnp.bfloat16)
    attended = jnp.einsum(
        "hqk,khd->qhd", weights_b, value_rows, preferred_element_type=jnp.float32
    ).astype(jnp.bfloat16)
    grad_weights = jnp.einsum(
        "qhd,khd->hqk", grad_attended, value_rows, preferred_element_type=jnp.float32
    )
    row_dots = jnp.sum(grad_attended.astype(jnp.float32) * attended.astype(jnp.float32), axis=2)
    grad_scores = (
        weights_f * (grad_weights - jnp.transpose(row_dots)[:, :, None]) * scaling
    ).astype(jnp.bfloat16)
    grad_query = jnp.einsum(
        "hqk,khd->qhd", grad_scores, key_rows, preferred_element_type=jnp.float32
    ).astype(jnp.bfloat16)
    grad_key = jnp.einsum(
        "hqk,qhd->khd", grad_scores, queries, preferred_element_type=jnp.float32
    ).astype(jnp.bfloat16)
    grad_value = jnp.einsum(
        "hqk,qhd->khd", weights_b, grad_attended, preferred_element_type=jnp.float32
    ).astype(jnp.bfloat16)
    return (attended, grad_query, grad_key, grad_value)


def local(layer_input, w_qkv, w_out, cotangent):
    qkv_block, out_block = (
        lax.all_gather(w_qkv, "inp", axis=2, tiled=True),
        lax.all_gather(w_out, "inp", axis=0, tiled=True),
    )
    wt_count = lax.axis_size("wt")
    head_cols = out_block.shape[0] // wt_count
    local_heads = head_cols // HEAD_DIM
    length = layer_input.shape[0]
    qkv_part = jnp.einsum("td,cde->tce", layer_input, qkv_block, preferred_element_type=jnp.float32)
    grad_part = jnp.einsum("td,ed->te", cotangent, out_block, preferred_element_type=jnp.float32)
    qkv_mine, grad_mine = (
        lax.psum_scatter(qkv_part, "wt", scatter_dimension=2, tiled=True),
        lax.psum_scatter(grad_part, "wt", scatter_dimension=1, tiled=True),
    )
    projected = qkv_mine.astype(jnp.bfloat16)
    queries = projected[:, 0].reshape(length, local_heads, HEAD_DIM)
    key_rows = projected[:, 1].reshape(length, local_heads, HEAD_DIM)
    value_rows = projected[:, 2].reshape(length, local_heads, HEAD_DIM)
    grad_attn = grad_mine.astype(jnp.bfloat16).reshape(length, local_heads, HEAD_DIM)
    attended, grad_query, grad_key, grad_value = attend_block(
        queries, key_rows, value_rows, grad_attn
    )
    grad_rows = jnp.stack([grad_query, grad_key, grad_value], axis=1).reshape(length, 3, head_cols)
    attended_rows = attended.reshape(length, head_cols)
    grad_all, attended_all = (
        lax.all_gather(grad_rows, "wt", axis=2, tiled=True),
        lax.all_gather(attended_rows, "wt", axis=1, tiled=True),
    )
    partial_input = jnp.einsum(
        "tce,cde->td", grad_all, qkv_block, preferred_element_type=jnp.float32
    )
    grad_input = lax.psum_scatter(partial_input, "out", scatter_dimension=1, tiled=True).astype(
        jnp.bfloat16
    )
    qkv_term = jnp.einsum("td,tce->cde", layer_input, grad_all, preferred_element_type=jnp.float32)
    out_term = jnp.einsum("te,td->ed", attended_all, cotangent, preferred_element_type=jnp.float32)
    qkv_total = lax.psum_scatter(
        qkv_term.astype(jnp.bfloat16), "inp", scatter_dimension=2, tiled=True
    )
    out_total = lax.psum_scatter(
        out_term.astype(jnp.bfloat16), "inp", scatter_dimension=0, tiled=True
    )
    return (grad_input, qkv_total, out_total)


BF = jnp.bfloat16
F32 = jnp.float32
N = HEAD_DIM
MESH = pl.DeviceIdType.MESH


def dot(a, b, dims):
    return lax.dot_general(a, b, (dims, ((), ())), preferred_element_type=F32)


def kernel(
    x_ref, w_ref, wo_ref, c_ref, gi_ref, gw_ref, go_ref,
    xo, co, part, from_core, from_x, mine, grads, att_t, gin, from_pair, from_cross,
    own_sum, far_sum, from_inp, acc_k, acc_v, send, recv,
):
    inp = lax.axis_index("inp")
    wt = lax.axis_index("wt")
    z = lax.axis_index("out")
    x_at, core = wt // 2, wt % 2
    length = x_ref.shape[0]
    width = x_ref.shape[1]
    cols = w_ref.shape[2]
    quarter = width // 4
    half = length // 2
    chunk = half // 2
    parity = z % 2
    z_pair, z_cross, z_far = z + 1 - 2 * parity, (z + 2) % 4, 3 - z
    inp_peer = {"inp": 1 - inp}
    core_peer = {"wt": wt + 1 - 2 * core}
    x_peer = {"wt": (wt + 2) % 4}
    pair_peer = {"out": z_pair}
    cross_peer = {"out": z_cross}

    barrier = pltpu.get_barrier_semaphore()
    for peer in (inp_peer, core_peer, x_peer, pair_peer, cross_peer):
        pl.semaphore_signal(barrier, inc=1, device_id=peer, device_id_type=MESH)
    pl.semaphore_wait(barrier, 5)

    used = [0]

    def copy(src, dst, peer):
        k = used[0]
        used[0] += 1
        return pltpu.make_async_remote_copy(
            src_ref=src, dst_ref=dst, send_sem=send.at[k], recv_sem=recv.at[k],
            device_id=peer, device_id_type=MESH,
        )

    def head(x, c):
        return pl.ds(pl.multiple_of((2 * x + c) * N, N), N)

    fetch, share = [], []
    for here, there in ((c_ref, co), (x_ref, xo)):
        for k in range(2):
            rows = pl.ds(pl.multiple_of(parity * half + k * chunk, 32), chunk)
            fetch.append(copy(here.at[rows], there.at[rows], inp_peer))
            share.append(copy(there.at[rows], there.at[rows], pair_peer))

    def forward(k):
        fetch[k].wait()
        share[k].start()
        if k + 2 < 4:
            fetch[k + 2].start()

    def project_out(acts):
        @pl.loop(0, 4)
        def _(t):
            rows = pl.ds(pl.multiple_of((t // 2) * half, half), half)
            n = cols // 2
            at = pl.ds(pl.multiple_of((t % 2) * n, n), n)
            part[3, rows, at] = dot(acts[rows, :], wo_ref[at, :], ((1,), (1,))).astype(BF)

    def project_in(acts):
        @pl.loop(0, 12)
        def _(t):
            rows = pl.ds(pl.multiple_of((t % 2) * half, half), half)
            n = cols // 2
            at = pl.ds(pl.multiple_of(((t // 2) % 2) * n, n), n)
            c = t // 4
            part[c, rows, at] = dot(acts[rows, :], w_ref[c, :, at], ((1,), (0,))).astype(BF)

    class Sequence:
        pass

    seqs = []
    for s in range(2):
        q = Sequence()
        q.core = [
            copy(part.at[:, :, head(x, 1 - core)], from_core.at[s, k], core_peer)
            for k, x in ((0, 1 - x_at), (1, x_at))
        ]
        q.across = copy(part.at[:, :, head(1 - x_at, core)], from_x.at[s], x_peer)
        own = grads.at[s, :, :, head(x_at, core)]
        other = grads.at[s, :, :, head(1 - x_at, core)]
        q.give_x = copy(own, own, x_peer)
        q.give_core = copy(own, own, core_peer)
        q.give_other = copy(other, other, core_peer)
        q.pair, q.cross = [], []
        for r in range(2):
            rows = pl.ds(r * half, half)
            q.pair.append(
                (
                    copy(gin.at[s, z_far, rows], from_pair.at[s, 0, rows], pair_peer),
                    copy(gin.at[s, z_pair, rows], from_pair.at[s, 1, rows], pair_peer),
                )
            )
            q.cross.append(copy(gin.at[s, z_cross, rows], from_cross.at[s, rows], cross_peer))
        seqs.append(q)
    back = [
        copy(far_sum.at[pl.ds(r * half, half)], from_inp.at[pl.ds(r * half, half)], inp_peer)
        for r in range(2)
    ]

    def scatter_start(s):
        for c in seqs[s].core:
            c.start()

    def scatter_across(s):
        for c in seqs[s].core:
            c.wait()
        at = head(1 - x_at, core)
        for j in range(4):
            total = part[j, :, at].astype(F32) + from_core[s, 0, j].astype(F32)
            part[j, :, at] = total.astype(BF)
        seqs[s].across.start()

    def scatter_end(s):
        at = head(x_at, core)
        seqs[s].across.wait()
        for j in range(4):
            total = part[j, :, at].astype(F32) + from_core[s, 1, j].astype(F32)
            mine[j] = (total + from_x[s, j].astype(F32)).astype(BF)

    def attention(s):
        scaling = 1.0 / math.sqrt(N)
        at = head(x_at, core)
        acc_k[...] = jnp.zeros_like(acc_k)
        acc_v[...] = jnp.zeros_like(acc_v)

        @pl.loop(0, length // N)
        def _(b):
            rows = pl.ds(pl.multiple_of(b * N, N), N)
            queries, grad = mine[0, rows, :], mine[3, rows, :]
            keys, values = mine[1], mine[2]
            scores = dot(queries, keys, ((1,), (1,))) * scaling
            row = lax.broadcasted_iota(jnp.int32, (N, length), 0) + b * N
            col = lax.broadcasted_iota(jnp.int32, (N, length), 1)
            scores = jnp.where(col <= row, scores, -1e30)
            powers = jnp.exp(scores - jnp.max(scores, axis=1, keepdims=True))
            probs = powers / jnp.sum(powers, axis=1, keepdims=True)
            probs_b = probs.astype(BF)
            attended = dot(probs_b, values, ((1,), (0,))).astype(BF)
            grad_probs = dot(grad, values, ((1,), (1,)))
            dots = jnp.sum(grad.astype(F32) * attended.astype(F32), axis=1, keepdims=True)
            grad_scores = (probs * (grad_probs - dots) * scaling).astype(BF)
            grads[s, 0, rows, at] = dot(grad_scores, keys, ((1,), (0,))).astype(BF)
            grads[s, 3, rows, at] = attended
            acc_k[...] += dot(grad_scores, queries, ((0,), (0,)))
            acc_v[...] += dot(probs_b, grad, ((0,), (0,)))

        grads[s, 1, :, at] = acc_k[...].astype(BF)
        grads[s, 2, :, at] = acc_v[...].astype(BF)

    def gather_start(s):
        seqs[s].give_x.start()
        seqs[s].give_core.start()

    def gather_pass(s):
        seqs[s].give_x.wait()
        seqs[s].give_other.start()

    def gather_end(s):
        seqs[s].give_core.wait()
        seqs[s].give_other.wait()

    def input_rows(s, r):
        rows = pl.ds(r * half, half)

        @pl.loop(0, 4)
        def _(k):
            at = pl.ds(pl.multiple_of(k * quarter, 64), quarter)
            total = dot(grads[s, 0, rows, :], w_ref[0, at, :], ((1,), (1,)))
            for c in (1, 2):
                total = total + dot(grads[s, c, rows, :], w_ref[c, at, :], ((1,), (1,)))
            gin[s, k, rows, :] = total.astype(BF)

        for c in seqs[s].pair[r]:
            c.start()

    def input_cross(s, r):
        rows = pl.ds(r * half, half)
        for c in seqs[s].pair[r]:
            c.wait()
        total = gin[s, z_cross, rows, :].astype(F32) + from_pair[s, 0, rows, :].astype(F32)
        gin[s, z_cross, rows, :] = total.astype(BF)
        seqs[s].cross[r].start()

    def input_end(s, r, out):
        rows = pl.ds(r * half, half)
        seqs[s].cross[r].wait()
        total = gin[s, z, rows, :].astype(F32) + from_pair[s, 1, rows, :].astype(F32)
        out[rows, :] = (total + from_cross[s, rows, :].astype(F32)).astype(out.dtype)

    def weight_in(s, acts):
        @pl.loop(0, width // 256)
        def _(m):
            at = pl.ds(pl.multiple_of(m * 256, 256), 256)
            turned = acts[:, at].T
            for c in range(3):
                term = dot(turned, grads[s, c], ((1,), (0,))).astype(BF)
                if s == 1:
                    term = (term.astype(F32) + gw_ref[c, at, :].astype(F32)).astype(BF)
                gw_ref[c, at, :] = term

    def weight_out(s, cots):
        att_t[...] = grads[s, 3].T

        @pl.loop(0, width // 256)
        def _(m):
            at = pl.ds(pl.multiple_of(m * 256, 256), 256)
            term = dot(att_t[...], cots[:, at], ((1,), (0,))).astype(BF)
            if s == 1:
                term = (term.astype(F32) + go_ref[:, at].astype(F32)).astype(BF)
            go_ref[:, at] = term

    fetch[0].start()
    fetch[1].start()
    project_out(c_ref)
    forward(0)
    project_in(x_ref)
    scatter_start(0)
    forward(1)
    scatter_across(0)
    scatter_end(0)
    attention(0)
    gather_start(0)
    forward(2)
    share[0].wait()
    share[1].wait()
    project_out(co)
    gather_pass(0)
    forward(3)
    gather_end(0)
    input_rows(0, 0)
    input_rows(0, 1)
    share[2].wait()
    share[3].wait()
    project_in(xo)
    scatter_start(1)
    weight_out(0, c_ref)
    scatter_across(1)
    weight_in(0, x_ref)
    input_cross(0, 0)
    input_cross(0, 1)
    scatter_end(1)
    attention(1)
    gather_start(1)
    input_end(0, 0, own_sum)
    input_end(0, 1, own_sum)
    gather_pass(1)
    gather_end(1)
    input_rows(1, 0)
    input_rows(1, 1)
    weight_out(1, co)
    input_cross(1, 0)
    weight_in(1, xo)
    input_cross(1, 1)
    for r in range(2):
        input_end(1, r, far_sum)
        back[r].start()
    for r in range(2):
        rows = pl.ds(r * half, half)
        back[r].wait()
        gi_ref[rows, :] = (own_sum[rows, :] + from_inp[rows, :].astype(F32)).astype(BF)


def local_fast(layer_input, w_qkv, w_out, cotangent):
    length, width = layer_input.shape
    cols = w_qkv.shape[2]
    quarter = width // 4
    vmem = pl.BlockSpec(memory_space=pltpu.VMEM)
    return pl.pallas_call(
        kernel,
        out_shape=[
            jax.ShapeDtypeStruct((length, quarter), BF),
            jax.ShapeDtypeStruct(w_qkv.shape, BF),
            jax.ShapeDtypeStruct(w_out.shape, BF),
        ],
        in_specs=[vmem] * 4,
        out_specs=[vmem] * 3,
        scratch_shapes=[
            pltpu.VMEM((length, width), BF),
            pltpu.VMEM((length, width), BF),
            pltpu.VMEM((4, length, cols), BF),
            pltpu.VMEM((2, 2, 4, length, N), BF),
            pltpu.VMEM((2, 4, length, N), BF),
            pltpu.VMEM((4, length, N), BF),
            pltpu.VMEM((2, 4, length, cols), BF),
            pltpu.VMEM((cols, length), BF),
            pltpu.VMEM((2, 4, length, quarter), BF),
            pltpu.VMEM((2, 2, length, quarter), BF),
            pltpu.VMEM((2, length, quarter), BF),
            pltpu.VMEM((length, quarter), F32),
            pltpu.VMEM((length, quarter), BF),
            pltpu.VMEM((length, quarter), BF),
            pltpu.VMEM((length, N), F32),
            pltpu.VMEM((length, N), F32),
            pltpu.SemaphoreType.DMA((40,)),
            pltpu.SemaphoreType.DMA((40,)),
        ],
        compiler_params=pltpu.CompilerParams(
            collective_id=0, has_side_effects=True, vmem_limit_bytes=62 * 2**20
        ),
    )(layer_input, w_qkv, w_out, cotangent)


def solution(mesh):
    sizes = dict(mesh.shape)
    fits = sizes["inp"] == 2 and sizes["wt"] == 4 and sizes["out"] == 4
    return jax.shard_map(
        local_fast if fits else local,
        mesh=mesh,
        in_specs=(
            P("inp", "wt"),
            P(None, "wt", ("inp", "out")),
            P(("inp", "out"), "wt"),
            P("inp", "wt"),
        ),
        out_specs=(P("inp", ("wt", "out")), P(None, "wt", ("inp", "out")), P(("inp", "out"), "wt")),
        check_vma=False,
    )
```

```python
import math

import jax
import jax.numpy as jnp
from jax import lax
from jax.experimental import pallas as pl
from jax.experimental.pallas import tpu as pltpu
from jax.sharding import PartitionSpec as P

HEAD_DIM = 128


def attend_block(queries, key_rows, value_rows, grad_attended):
    length = queries.shape[0]
    scaling = 1.0 / math.sqrt(queries.shape[2])
    scores = (
        jnp.einsum("qhd,khd->hqk", queries, key_rows, preferred_element_type=jnp.float32) * scaling
    )
    row_index = jnp.arange(length)[:, None]
    col_index = jnp.arange(length)[None, :]
    causal = col_index <= row_index
    scores = jnp.where(causal[None], scores, -1e30)
    largest = jnp.max(scores, axis=2, keepdims=True)
    powers = jnp.exp(scores - largest)
    weights_f = powers / jnp.sum(powers, axis=2, keepdims=True)
    weights_b = weights_f.astype(jnp.bfloat16)
    attended = jnp.einsum(
        "hqk,khd->qhd", weights_b, value_rows, preferred_element_type=jnp.float32
    ).astype(jnp.bfloat16)
    grad_weights = jnp.einsum(
        "qhd,khd->hqk", grad_attended, value_rows, preferred_element_type=jnp.float32
    )
    row_dots = jnp.sum(grad_attended.astype(jnp.float32) * attended.astype(jnp.float32), axis=2)
    grad_scores = (
        weights_f * (grad_weights - jnp.transpose(row_dots)[:, :, None]) * scaling
    ).astype(jnp.bfloat16)
    grad_query = jnp.einsum(
        "hqk,khd->qhd", grad_scores, key_rows, preferred_element_type=jnp.float32
    ).astype(jnp.bfloat16)
    grad_key = jnp.einsum(
        "hqk,qhd->khd", grad_scores, queries, preferred_element_type=jnp.float32
    ).astype(jnp.bfloat16)
    grad_value = jnp.einsum(
        "hqk,qhd->khd", weights_b, grad_attended, preferred_element_type=jnp.float32
    ).astype(jnp.bfloat16)
    return (attended, grad_query, grad_key, grad_value)


def local(layer_input, w_qkv, w_out, cotangent):
    qkv_block, out_block = (
        lax.all_gather(w_qkv, "inp", axis=2, tiled=True),
        lax.all_gather(w_out, "inp", axis=0, tiled=True),
    )
    wt_count = lax.axis_size("wt")
    head_cols = out_block.shape[0] // wt_count
    local_heads = head_cols // HEAD_DIM
    length = layer_input.shape[0]
    qkv_part = jnp.einsum("td,cde->tce", layer_input, qkv_block, preferred_element_type=jnp.float32)
    grad_part = jnp.einsum("td,ed->te", cotangent, out_block, preferred_element_type=jnp.float32)
    qkv_mine, grad_mine = (
        lax.psum_scatter(qkv_part, "wt", scatter_dimension=2, tiled=True),
        lax.psum_scatter(grad_part, "wt", scatter_dimension=1, tiled=True),
    )
    projected = qkv_mine.astype(jnp.bfloat16)
    queries = projected[:, 0].reshape(length, local_heads, HEAD_DIM)
    key_rows = projected[:, 1].reshape(length, local_heads, HEAD_DIM)
    value_rows = projected[:, 2].reshape(length, local_heads, HEAD_DIM)
    grad_attn = grad_mine.astype(jnp.bfloat16).reshape(length, local_heads, HEAD_DIM)
    attended, grad_query, grad_key, grad_value = attend_block(
        queries, key_rows, value_rows, grad_attn
    )
    grad_rows = jnp.stack([grad_query, grad_key, grad_value], axis=1).reshape(length, 3, head_cols)
    attended_rows = attended.reshape(length, head_cols)
    grad_all, attended_all = (
        lax.all_gather(grad_rows, "wt", axis=2, tiled=True),
        lax.all_gather(attended_rows, "wt", axis=1, tiled=True),
    )
    partial_input = jnp.einsum(
        "tce,cde->td", grad_all, qkv_block, preferred_element_type=jnp.float32
    )
    grad_input = lax.psum_scatter(partial_input, "out", scatter_dimension=1, tiled=True).astype(
        jnp.bfloat16
    )
    qkv_term = jnp.einsum("td,tce->cde", layer_input, grad_all, preferred_element_type=jnp.float32)
    out_term = jnp.einsum("te,td->ed", attended_all, cotangent, preferred_element_type=jnp.float32)
    qkv_total = lax.psum_scatter(
        qkv_term.astype(jnp.bfloat16), "inp", scatter_dimension=2, tiled=True
    )
    out_total = lax.psum_scatter(
        out_term.astype(jnp.bfloat16), "inp", scatter_dimension=0, tiled=True
    )
    return (grad_input, qkv_total, out_total)


BF = jnp.bfloat16
F32 = jnp.float32
N = HEAD_DIM
MESH = pl.DeviceIdType.MESH


def dot(a, b, dims):
    return lax.dot_general(a, b, (dims, ((), ())), preferred_element_type=F32)


def kernel(
    x_ref, w_ref, wo_ref, c_ref, gi_ref, gw_ref, go_ref,
    xo, co, part, from_core, from_x, mine, grads, att_t, gin, from_pair, from_cross,
    own_sum, far_sum, from_inp, acc_k, acc_v, send, recv,
):
    inp = lax.axis_index("inp")
    wt = lax.axis_index("wt")
    z = lax.axis_index("out")
    x_at, core = wt // 2, wt % 2
    length = x_ref.shape[0]
    width = x_ref.shape[1]
    cols = w_ref.shape[2]
    quarter = width // 4
    half = length // 2
    chunk = half // 2
    parity = z % 2
    z_pair, z_cross, z_far = z + 1 - 2 * parity, (z + 2) % 4, 3 - z
    inp_peer = {"inp": 1 - inp}
    core_peer = {"wt": wt + 1 - 2 * core}
    x_peer = {"wt": (wt + 2) % 4}
    pair_peer = {"out": z_pair}
    cross_peer = {"out": z_cross}

    barrier = pltpu.get_barrier_semaphore()
    for peer in (inp_peer, core_peer, x_peer, pair_peer, cross_peer):
        pl.semaphore_signal(barrier, inc=1, device_id=peer, device_id_type=MESH)
    pl.semaphore_wait(barrier, 5)

    used = [0]

    def copy(src, dst, peer):
        k = used[0]
        used[0] += 1
        return pltpu.make_async_remote_copy(
            src_ref=src, dst_ref=dst, send_sem=send.at[k], recv_sem=recv.at[k],
            device_id=peer, device_id_type=MESH,
        )

    def head(x, c):
        return pl.ds(pl.multiple_of((2 * x + c) * N, N), N)

    fetch, share = [], []
    for here, there in ((c_ref, co), (x_ref, xo)):
        for k in range(2):
            rows = pl.ds(pl.multiple_of(parity * half + k * chunk, 32), chunk)
            fetch.append(copy(here.at[rows], there.at[rows], inp_peer))
            share.append(copy(there.at[rows], there.at[rows], pair_peer))

    def forward(k):
        fetch[k].wait()
        share[k].start()
        if k + 2 < 4:
            fetch[k + 2].start()

    def project_out(acts):
        @pl.loop(0, 4)
        def _(t):
            rows = pl.ds(pl.multiple_of((t // 2) * half, half), half)
            n = cols // 2
            at = pl.ds(pl.multiple_of((t % 2) * n, n), n)
            part[3, rows, at] = dot(acts[rows, :], wo_ref[at, :], ((1,), (1,))).astype(BF)

    def project_in(acts):
        @pl.loop(0, 12)
        def _(t):
            rows = pl.ds(pl.multiple_of((t % 2) * half, half), half)
            n = cols // 2
            at = pl.ds(pl.multiple_of(((t // 2) % 2) * n, n), n)
            c = t // 4
            part[c, rows, at] = dot(acts[rows, :], w_ref[c, :, at], ((1,), (0,))).astype(BF)

    class Sequence:
        pass

    seqs = []
    for s in range(2):
        q = Sequence()
        q.core = [
            copy(part.at[:, :, head(x, 1 - core)], from_core.at[s, k], core_peer)
            for k, x in ((0, 1 - x_at), (1, x_at))
        ]
        q.across = copy(part.at[:, :, head(1 - x_at, core)], from_x.at[s], x_peer)
        own = grads.at[s, :, :, head(x_at, core)]
        other = grads.at[s, :, :, head(1 - x_at, core)]
        q.give_x = copy(own, own, x_peer)
        q.give_core = copy(own, own, core_peer)
        q.give_other = copy(other, other, core_peer)
        q.pair, q.cross = [], []
        for r in range(2):
            rows = pl.ds(r * half, half)
            q.pair.append(
                (
                    copy(gin.at[s, z_far, rows], from_pair.at[s, 0, rows], pair_peer),
                    copy(gin.at[s, z_pair, rows], from_pair.at[s, 1, rows], pair_peer),
                )
            )
            q.cross.append(copy(gin.at[s, z_cross, rows], from_cross.at[s, rows], cross_peer))
        seqs.append(q)
    back = [
        copy(far_sum.at[pl.ds(r * half, half)], from_inp.at[pl.ds(r * half, half)], inp_peer)
        for r in range(2)
    ]

    def scatter_start(s):
        for c in seqs[s].core:
            c.start()

    def scatter_across(s):
        for c in seqs[s].core:
            c.wait()
        at = head(1 - x_at, core)
        for j in range(4):
            total = part[j, :, at].astype(F32) + from_core[s, 0, j].astype(F32)
            part[j, :, at] = total.astype(BF)
        seqs[s].across.start()

    def scatter_end(s):
        at = head(x_at, core)
        seqs[s].across.wait()
        for j in range(4):
            total = part[j, :, at].astype(F32) + from_core[s, 1, j].astype(F32)
            mine[j] = (total + from_x[s, j].astype(F32)).astype(BF)

    def attention(s):
        scaling = 1.0 / math.sqrt(N)
        at = head(x_at, core)
        acc_k[...] = jnp.zeros_like(acc_k)
        acc_v[...] = jnp.zeros_like(acc_v)

        @pl.loop(0, length // N)
        def _(b):
            rows = pl.ds(pl.multiple_of(b * N, N), N)
            queries, grad = mine[0, rows, :], mine[3, rows, :]
            keys, values = mine[1], mine[2]
            scores = dot(queries, keys, ((1,), (1,))) * scaling
            row = lax.broadcasted_iota(jnp.int32, (N, length), 0) + b * N
            col = lax.broadcasted_iota(jnp.int32, (N, length), 1)
            scores = jnp.where(col <= row, scores, -1e30)
            powers = jnp.exp(scores - jnp.max(scores, axis=1, keepdims=True))
            probs = powers / jnp.sum(powers, axis=1, keepdims=True)
            probs_b = probs.astype(BF)
            attended = dot(probs_b, values, ((1,), (0,))).astype(BF)
            grad_probs = dot(grad, values, ((1,), (1,)))
            dots = jnp.sum(grad.astype(F32) * attended.astype(F32), axis=1, keepdims=True)
            grad_scores = (probs * (grad_probs - dots) * scaling).astype(BF)
            grads[s, 0, rows, at] = dot(grad_scores, keys, ((1,), (0,))).astype(BF)
            grads[s, 3, rows, at] = attended
            acc_k[...] += dot(grad_scores, queries, ((0,), (0,)))
            acc_v[...] += dot(probs_b, grad, ((0,), (0,)))

        grads[s, 1, :, at] = acc_k[...].astype(BF)
        grads[s, 2, :, at] = acc_v[...].astype(BF)

    def gather_start(s):
        seqs[s].give_x.start()
        seqs[s].give_core.start()

    def gather_pass(s):
        seqs[s].give_x.wait()
        seqs[s].give_other.start()

    def gather_end(s):
        seqs[s].give_core.wait()
        seqs[s].give_other.wait()

    def input_all(s):
        for order, k in enumerate((z_far, z_cross, z_pair, z)):
            at = pl.ds(pl.multiple_of(k * quarter, 64), quarter)
            for r in range(2):
                rows = pl.ds(r * half, half)
                total = dot(grads[s, 0, rows, :], w_ref[0, at, :], ((1,), (1,)))
                for c in (1, 2):
                    total = total + dot(grads[s, c, rows, :], w_ref[c, at, :], ((1,), (1,)))
                gin[s, k, rows, :] = total.astype(BF)
                if order % 2 == 0:
                    seqs[s].pair[r][order // 2].start()

    def input_cross(s, r):
        rows = pl.ds(r * half, half)
        seqs[s].pair[r][0].wait()
        total = gin[s, z_cross, rows, :].astype(F32) + from_pair[s, 0, rows, :].astype(F32)
        gin[s, z_cross, rows, :] = total.astype(BF)
        seqs[s].cross[r].start()

    def input_end(s, r, out):
        rows = pl.ds(r * half, half)
        seqs[s].pair[r][1].wait()
        seqs[s].cross[r].wait()
        total = gin[s, z, rows, :].astype(F32) + from_pair[s, 1, rows, :].astype(F32)
        out[rows, :] = (total + from_cross[s, rows, :].astype(F32)).astype(out.dtype)

    def weight_in(s, acts):
        @pl.loop(0, width // 256)
        def _(m):
            at = pl.ds(pl.multiple_of(m * 256, 256), 256)
            turned = acts[:, at].T
            for c in range(3):
                term = dot(turned, grads[s, c], ((1,), (0,))).astype(BF)
                if s == 1:
                    term = (term.astype(F32) + gw_ref[c, at, :].astype(F32)).astype(BF)
                gw_ref[c, at, :] = term

    def weight_out(s, cots):
        att_t[...] = grads[s, 3].T

        @pl.loop(0, width // 256)
        def _(m):
            at = pl.ds(pl.multiple_of(m * 256, 256), 256)
            term = dot(att_t[...], cots[:, at], ((1,), (0,))).astype(BF)
            if s == 1:
                term = (term.astype(F32) + go_ref[:, at].astype(F32)).astype(BF)
            go_ref[:, at] = term

    fetch[0].start()
    fetch[1].start()
    project_out(c_ref)
    forward(0)
    project_in(x_ref)
    scatter_start(0)
    forward(1)
    scatter_across(0)
    scatter_end(0)
    attention(0)
    gather_start(0)
    forward(2)
    share[0].wait()
    share[1].wait()
    project_out(co)
    gather_pass(0)
    forward(3)
    gather_end(0)
    weight_out(0, c_ref)
    share[2].wait()
    share[3].wait()
    project_in(xo)
    scatter_start(1)
    input_all(0)
    scatter_across(1)
    weight_in(0, x_ref)
    input_cross(0, 0)
    input_cross(0, 1)
    scatter_end(1)
    attention(1)
    gather_start(1)
    input_end(0, 0, own_sum)
    input_end(0, 1, own_sum)
    gather_pass(1)
    gather_end(1)
    input_all(1)
    input_cross(1, 0)
    weight_out(1, co)
    input_cross(1, 1)
    weight_in(1, xo)
    for r in range(2):
        input_end(1, r, far_sum)
        back[r].start()
    for r in range(2):
        rows = pl.ds(r * half, half)
        back[r].wait()
        gi_ref[rows, :] = (own_sum[rows, :] + from_inp[rows, :].astype(F32)).astype(BF)


def local_fast(layer_input, w_qkv, w_out, cotangent):
    length, width = layer_input.shape
    cols = w_qkv.shape[2]
    quarter = width // 4
    vmem = pl.BlockSpec(memory_space=pltpu.VMEM)
    return pl.pallas_call(
        kernel,
        out_shape=[
            jax.ShapeDtypeStruct((length, quarter), BF),
            jax.ShapeDtypeStruct(w_qkv.shape, BF),
            jax.ShapeDtypeStruct(w_out.shape, BF),
        ],
        in_specs=[vmem] * 4,
        out_specs=[vmem] * 3,
        scratch_shapes=[
            pltpu.VMEM((length, width), BF),
            pltpu.VMEM((length, width), BF),
            pltpu.VMEM((4, length, cols), BF),
            pltpu.VMEM((2, 2, 4, length, N), BF),
            pltpu.VMEM((2, 4, length, N), BF),
            pltpu.VMEM((4, length, N), BF),
            pltpu.VMEM((2, 4, length, cols), BF),
            pltpu.VMEM((cols, length), BF),
            pltpu.VMEM((2, 4, length, quarter), BF),
            pltpu.VMEM((2, 2, length, quarter), BF),
            pltpu.VMEM((2, length, quarter), BF),
            pltpu.VMEM((length, quarter), F32),
            pltpu.VMEM((length, quarter), BF),
            pltpu.VMEM((length, quarter), BF),
            pltpu.VMEM((length, N), F32),
            pltpu.VMEM((length, N), F32),
            pltpu.SemaphoreType.DMA((40,)),
            pltpu.SemaphoreType.DMA((40,)),
        ],
        compiler_params=pltpu.CompilerParams(
            collective_id=0, has_side_effects=True, vmem_limit_bytes=62 * 2**20
        ),
    )(layer_input, w_qkv, w_out, cotangent)


def solution(mesh):
    sizes = dict(mesh.shape)
    fits = sizes["inp"] == 2 and sizes["wt"] == 4 and sizes["out"] == 4
    return jax.shard_map(
        local_fast if fits else local,
        mesh=mesh,
        in_specs=(
            P("inp", "wt"),
            P(None, "wt", ("inp", "out")),
            P(("inp", "out"), "wt"),
            P("inp", "wt"),
        ),
        out_specs=(P("inp", ("wt", "out")), P(None, "wt", ("inp", "out")), P(("inp", "out"), "wt")),
        check_vma=False,
    )
```
